32 devices in a mesh: req: 2 (over x), hst: 16 (over z, y, core).
Axes of the slice: x: 2, y: 2, z: 4, core: 2. Of those that a mesh axis runs over, the one named last changes fastest.
Arguments:
- ctx_q: bfloat16 [4096, 4096], P(('req', 'hst')), parts along dimension 0, may hold values from -24 to 24
- ctx_k: bfloat16 [4096, 512], P(('req', 'hst')), parts along dimension 0, may hold values from -8 to 8
- ctx_v: bfloat16 [4096, 512], P(('req', 'hst')), parts along dimension 0, may hold values from -6 to 6
- ask_q: bfloat16 [64, 4096], P(('req', 'hst')), parts along dimension 0, may hold values from -24 to 24
- ask_k: bfloat16 [64, 512], P(('req', 'hst')), parts along dimension 0, may hold values from -9 to 9
- ask_v: bfloat16 [64, 512], P(('req', 'hst')), parts along dimension 0, may hold values from -6 to 6
- valid: int32 [32], P(('req', 'hst')), parts along dimension 0, may hold values from 64 to 128, as said below
Outputs:
- ctx_out: bfloat16 [4096, 4096], P(('req', 'hst')), parts along dimension 0
- ask_out: bfloat16 [64, 4096], P(('req', 'hst')), parts along dimension 0
The draws below stay inside these ranges and needn't reach their ends.
There are 2 independent parts, one for each index of `req`. The reference program is written for one: setup_inputs(seed, part) draws one part's arguments, and reference() takes and returns one part's arrays. A program takes and returns all parts, laid end to end along the dimension named above; each array names one. Nothing has to cross between parts.
Inputs may be any that keep to these rules, and one draw needn't show every extreme that they name: `valid`: block 0, the anchor, is always full.
All inputs are finite; a program needn't handle non-finite values.
Results may differ from the reference program's by a relative error of at most 0.0029.
Values may be sent and summed in bfloat16 or wider, within the bound.
No kernel may reach another device: no remote copies, remote signals or barrier semaphores. Data moves between devices by JAX's collectives and lax.ppermute only.
A program may use at most 320 MiB of HBM per device.

```python
import math
import jax
import jax.numpy as jnp
from jax import lax

H = 32
KVH = 4
DH = 128
BLOCK = 128
TOKENS = 2048
QLEN = 32
N_HST = 16


def draw_ctx_q(key, part):
    values = jnp.clip(jax.random.normal(jax.random.fold_in(key, 1), (TOKENS, H * DH)) * 2.5, -10.0, 10.0)
    return values.astype(jnp.bfloat16)


def draw_ctx_k(key, part):
    values = jnp.clip(jax.random.normal(jax.random.fold_in(key, 5), (TOKENS, KVH * DH)), -6.0, 6.0)
    return values.astype(jnp.bfloat16)


def draw_ask_q(key, part):
    values = jnp.clip(jax.random.normal(jax.random.fold_in(key, 11), (QLEN, H * DH)) * 2.5, -10.0, 10.0)
    return values.astype(jnp.bfloat16)


def draw_valid(key, part):
    host_count = TOKENS // BLOCK
    counts = jax.random.randint(jax.random.fold_in(key, 21), (host_count,), BLOCK // 2, BLOCK + 1)
    lowest = jax.random.randint(jax.random.fold_in(key, 22), (), 1, host_count)
    counts = counts.at[lowest].set(BLOCK // 2)
    counts = counts.at[0].set(BLOCK)
    return counts.astype(jnp.int32)


def block_scale(key, dims, cuts, smallest, high):
    loudness = 1.0
    for axis_at, parts in cuts:
        steps = jax.random.uniform(jax.random.fold_in(jax.random.fold_in(key, 6), axis_at), (parts,), jnp.float32, smallest / len(cuts), high / len(cuts))
        loudness = loudness * jnp.repeat(jnp.exp(steps), dims[axis_at] // parts).reshape((-1,) + (1,) * (len(dims) - 1 - axis_at))
    return loudness


def normal_values(stream_key, shape, spread, limit, cuts=(), held_as=jnp.bfloat16):
    loudness = block_scale(stream_key, shape, cuts, -0.22, 0.18) if cuts else 1.0
    result = jax.random.normal(stream_key, shape, jnp.float32) * spread * loudness
    return jnp.minimum(jnp.maximum(result, -limit), limit).astype(held_as)


def setup_inputs(seed: int = 0, part: int = 0) -> dict:
    seeds = jax.random.split(jax.random.key(seed), 8)
    part_splits = jax.random.split(jax.random.fold_in(seeds[7], part), 8)
    ctx_q = draw_ctx_q(jax.random.fold_in(jax.random.fold_in(seeds[7], part), 71), part)
    ctx_k = draw_ctx_k(jax.random.fold_in(jax.random.fold_in(seeds[7], part), 71), part)
    ctx_v = normal_values(part_splits[2], (TOKENS, KVH * DH), 1.0, 6.0, ((0, 16),))
    ask_q = draw_ask_q(jax.random.fold_in(jax.random.fold_in(seeds[7], part), 71), part)
    ask_k = normal_values(part_splits[4], (QLEN, KVH * DH), 1.5, 9.0, ((0, 16),))
    ask_v = normal_values(part_splits[5], (QLEN, KVH * DH), 1.0, 6.0, ((0, 16),))
    valid = draw_valid(jax.random.fold_in(jax.random.fold_in(seeds[7], part), 71), part)
    return dict(ctx_q=ctx_q, ctx_k=ctx_k, ctx_v=ctx_v, ask_q=ask_q, ask_k=ask_k, ask_v=ask_v, valid=valid)


def partial_attend(queries, key_rows, value_rows, visible):
    row_count = queries.shape[0]
    span_count = key_rows.shape[0]
    group_size = H // KVH
    query_f = queries.astype(jnp.float32).reshape(row_count, KVH, group_size, DH)
    key_f = key_rows.astype(jnp.float32).reshape(span_count, KVH, DH)
    value_f = value_rows.astype(jnp.float32).reshape(span_count, KVH, DH)
    scores = jnp.einsum('rkgd,skd->rkgs', query_f, key_f) * (1.0 / math.sqrt(DH))
    scores = jnp.where(visible[:, None, None, :], scores, -jnp.inf)
    row_max = lax.optimization_barrier(jnp.max(scores, axis=-1))
    expon = jnp.exp(scores - row_max[..., None])
    row_sum = lax.optimization_barrier(jnp.sum(expon, axis=-1))
    rounded = lax.optimization_barrier(expon.astype(jnp.bfloat16)).astype(jnp.float32)
    mixed = jnp.einsum('rkgs,skd->rkgd', rounded, value_f)
    return (row_max.reshape(row_count, H), row_sum.reshape(row_count, H), mixed.reshape(row_count, H * DH))

def weigh(values, factor):
    shape = values.shape
    return (values.reshape(shape[:-1] + (H, DH)) * factor[..., None]).reshape(shape)

def reference(ctx_q, ctx_k, ctx_v, ask_q, ask_k, ask_v, valid):
    local = jnp.arange(BLOCK, dtype=jnp.int32)
    anchor_k = ctx_k[:BLOCK]
    anchor_v = ctx_v[:BLOCK]

    def context_block(block_index):
        start = (block_index * BLOCK).astype(jnp.int32)
        queries = lax.dynamic_slice_in_dim(ctx_q, start, BLOCK, 0)
        own_k = lax.dynamic_slice_in_dim(ctx_k, start, BLOCK, 0)
        own_v = lax.dynamic_slice_in_dim(ctx_v, start, BLOCK, 0)
        valid_count = valid[block_index]
        own_visible = (local[None, :] <= local[:, None]) & (local[None, :] < valid_count)
        anchor_visible = jnp.broadcast_to(block_index > 0, (BLOCK, BLOCK))
        visible = jnp.concatenate([anchor_visible, own_visible], axis=1)
        row_max, row_sum, mixed = partial_attend(queries, jnp.concatenate([anchor_k, own_k], 0), jnp.concatenate([anchor_v, own_v], 0), visible)
        normed = weigh(mixed, 1.0 / row_sum)
        return jnp.where(local[:, None] < valid_count, normed, 0.0).astype(jnp.bfloat16)
    ctx_out = lax.map(context_block, jnp.arange(N_HST, dtype=jnp.int32)).reshape(TOKENS, H * DH)
    query_pos = jnp.arange(QLEN, dtype=jnp.int32)
    causal = query_pos[None, :] <= query_pos[:, None]

    def host_step(carry, block_index):
        best, total, summed = carry
        start = (block_index * BLOCK).astype(jnp.int32)
        own_k = lax.dynamic_slice_in_dim(ctx_k, start, BLOCK, 0)
        own_v = lax.dynamic_slice_in_dim(ctx_v, start, BLOCK, 0)
        valid_count = valid[block_index]
        visible = jnp.concatenate([jnp.broadcast_to(local[None, :] < valid_count, (QLEN, BLOCK)), causal & (block_index == N_HST - 1)], axis=1)
        row_max, row_sum, mixed = partial_attend(ask_q, jnp.concatenate([own_k, ask_k], 0), jnp.concatenate([own_v, ask_v], 0), visible)
        new_best = jnp.maximum(best, row_max)
        old_weight = jnp.exp(best - new_best)
        new_weight = jnp.exp(row_max - new_best)
        return ((new_best, total * old_weight + row_sum * new_weight, weigh(summed, old_weight) + weigh(mixed, new_weight)), None)
    start_carry = (jnp.full((QLEN, H), -jnp.inf, jnp.float32), jnp.zeros((QLEN, H), jnp.float32), jnp.zeros((QLEN, H * DH), jnp.float32))
    (best, total, summed), _ = lax.scan(host_step, start_carry, jnp.arange(N_HST, dtype=jnp.int32))
    ask_out = weigh(summed, 1.0 / total).astype(jnp.bfloat16)
    return (ctx_out, ask_out)
```

```python
import functools
import math

import jax
import jax.numpy as jnp
from jax import lax
from jax.experimental import pallas as pl
from jax.experimental.pallas import tpu as pltpu
from jax.sharding import PartitionSpec as P

H = 32
KVH = 4
DH = 128
HEADS = H // KVH
SUB = 16
SCALE = 1.0 / math.sqrt(DH)
NEG = -math.inf
COSTS = {'ask': 20000000000.0, 'merge': 20000000000.0, 'regroup': 10000000000.0, 'gate': 20000000000.0}
BF16 = jnp.bfloat16
F32 = jnp.float32
VMEM = pl.BlockSpec(memory_space=pltpu.VMEM)
SMEM = pl.BlockSpec(memory_space=pltpu.SMEM)
HBM = pl.BlockSpec(memory_space=pltpu.HBM)


def round_up(value, step):
    return -(-value // step) * step


def params(**more):
    return pltpu.CompilerParams(vmem_limit_bytes=32 * 2**20, **more)


def dot_nt(a, b):
    return lax.dot_general(a, b, (((1,), (1,)), ((), ())), preferred_element_type=F32)


def dot_nn(a, b):
    return lax.dot_general(a, b, (((1,), (0,)), ((), ())), preferred_element_type=F32)


def head_columns(head, width=DH):
    return pl.ds(pl.multiple_of(head * width, width), width)


def diagonal(rows):
    shape = (rows, DH)
    return lax.broadcasted_iota(jnp.int32, shape, 0) == lax.broadcasted_iota(jnp.int32, shape, 1)


def place():
    return lax.rem(lax.axis_index("hst"), KVH)


def gate_kernel(mark_ref):
    mark_ref[...] = jnp.zeros(mark_ref.shape, F32)


def pack_kernel(valid_ref, q_ref, ak_ref, av_ref, k_ref, v_ref, earlier_ref, *refs):
    del earlier_ref
    q_outs, kv_outs = refs[:KVH], refs[KVH:]
    tokens = q_ref.shape[0]
    block = k_ref.shape[0]
    me = place()
    count = jnp.full((1, DH), valid_ref[0], jnp.int32).astype(F32)
    for x in range(KVH):
        head = jnp.bitwise_xor(me, x)
        q = q_ref[:, head_columns(head, HEADS * DH)].astype(F32)
        rows = [q[t : t + 1, h * DH : (h + 1) * DH] for t in range(tokens) for h in range(HEADS)]
        rows.append(ak_ref[:, head_columns(head)].astype(F32))
        rows.append(av_ref[:, head_columns(head)].astype(F32))
        rows.append(count)
        spare = q_outs[x].shape[0] - tokens * HEADS - 2 * tokens - 1
        if spare:
            rows.append(jnp.zeros((spare, DH), F32))
        q_outs[x][...] = jnp.concatenate(rows, axis=0).astype(BF16)
    for x in range(KVH):
        cols = head_columns(jnp.bitwise_xor(me, x))
        kv_outs[x][:block, :] = k_ref[:, cols]
        kv_outs[x][block:, :] = v_ref[:, cols]


def regroup_kernel(tokens, *refs):
    pieces, out_ref = refs[:KVH], refs[-1]
    rows_q = tokens * HEADS
    extra = []
    for x in range(KVH):
        out_ref[x * rows_q : (x + 1) * rows_q, :] = pieces[x][:rows_q, :]
        extra.append(pieces[x][rows_q:, :].astype(F32)[: 2 * tokens, :])
    out_ref[KVH * rows_q :, :] = jnp.concatenate(extra, axis=0).astype(BF16)


def ask_kernel(hosts, tokens, *refs):
    groups = hosts // KVH
    z_refs, q_refs, kv_refs = refs[:groups], refs[groups : groups + KVH], refs[groups + KVH :]
    kv_refs, out_ref = kv_refs[:KVH], kv_refs[KVH]
    rows_q = tokens * HEADS
    rows_z = KVH * rows_q
    me = place()
    group = lax.axis_index("hst") // KVH
    last_group = group == groups - 1
    block = kv_refs[0].shape[0] // 2
    total_rows = groups * rows_z
    q = jnp.concatenate([z[:rows_z, :] for z in z_refs], axis=0)
    extra = jnp.concatenate([z[rows_z:, :] for z in z_refs], axis=0)
    asks = hosts * tokens

    def token_of(index, per_group, per_host, per_token):
        from_group = jnp.bitwise_xor(index // per_group, group)
        from_place = jnp.bitwise_xor(index % per_group // per_host, me)
        return (from_group * KVH + from_place) * tokens + index % per_host // per_token

    per_host = 2 * tokens
    wide = groups * KVH * per_host
    u = lax.broadcasted_iota(jnp.int32, (asks, wide), 0)
    c = lax.broadcasted_iota(jnp.int32, (1, wide), 1)
    part = c % per_host
    token = token_of(c - part + part % tokens, KVH * per_host, per_host, 1)
    token_k = jnp.where(part < tokens, token, -1)
    token_v = jnp.where(part < tokens, -1, token)
    ask_k = dot_nn(jnp.where(u == token_k, 1.0, 0.0).astype(BF16), extra).astype(BF16)
    ask_v = dot_nn(jnp.where(u == token_v, 1.0, 0.0).astype(BF16), extra).astype(BF16)

    row = lax.broadcasted_iota(jnp.int32, (total_rows, 1), 0)
    row_token = token_of(row, rows_z, rows_q, HEADS)
    col = lax.broadcasted_iota(jnp.int32, (total_rows, asks), 1)
    s = dot_nt(q, ask_k) * SCALE
    ask_scores = jnp.where((col <= row_token) & last_group, s, NEG)
    ask_best = jnp.max(ask_scores, axis=1, keepdims=True)
    ask_shift = ask_best
    lane = lax.broadcasted_iota(jnp.int32, (1, block), 1).astype(F32)
    tops, sums, mixes = [], [], []
    for x in range(KVH):
        s = dot_nt(q, kv_refs[x][:block, :]) * SCALE
        is_last = last_group & (jnp.bitwise_xor(me, x) == KVH - 1)
        info = q_refs[x][rows_q:, :].astype(F32)
        count = info[2 * tokens : 2 * tokens + 1, :1]
        s = jnp.where(lane < count, s, NEG)
        top = jnp.max(s, axis=1, keepdims=True)
        top = jnp.where(is_last, jnp.maximum(top, ask_best), top)
        ask_shift = jnp.where(is_last, top, ask_shift)
        e = jnp.exp(s - top)
        tops.append(top)
        sums.append(jnp.sum(e, axis=1, keepdims=True))
        mixes.append(dot_nn(e.astype(BF16), kv_refs[x][block:, :]))
    ask_shift = jnp.where(last_group, ask_shift, 0.0)
    e = jnp.exp(ask_scores - ask_shift)
    sums.append(jnp.sum(e, axis=1, keepdims=True))
    mixes.append(dot_nn(e.astype(BF16), ask_v))
    best = functools.reduce(jnp.maximum, tops).astype(BF16).astype(F32)
    factors = [jnp.exp(top - best) for top in tops]
    factors.append(jnp.where(last_group, jnp.exp(ask_shift - best), 0.0))
    total = functools.reduce(jnp.add, [f * part for f, part in zip(factors, sums)])
    mixed = functools.reduce(jnp.add, [f * part for f, part in zip(factors, mixes)])
    mask = diagonal(rows_q)
    total_high = total.astype(BF16).astype(F32)
    mixed_high = mixed.astype(BF16).astype(F32)
    stats = (best, total_high, total - total_high)
    spare = jnp.zeros((out_ref.shape[1] - 2 * rows_q - len(stats), DH), F32)
    for d in range(groups):
        for x in range(KVH):
            at = d * rows_z + x * rows_q
            rows = slice(at, at + rows_q)
            to = jnp.bitwise_xor(group, d) * KVH + jnp.bitwise_xor(me, x)
            pieces = [mixed_high[rows], mixed[rows] - mixed_high[rows]]
            for stat in stats:
                pieces.append(jnp.sum(jnp.where(mask, stat[rows], 0.0), axis=0, keepdims=True))
            out_ref[to] = jnp.concatenate([*pieces, spare], axis=0).astype(BF16)


def merge_kernel(recv_ref, out_ref):
    tokens = out_ref.shape[0]
    rows_q = tokens * HEADS
    groups = recv_ref.shape[0] // KVH
    mask = diagonal(rows_q)
    lines = [[] for _ in range(tokens)]
    for g in range(KVH):
        parts = [recv_ref[j * KVH + g].astype(F32) for j in range(groups)]

        tops = [part[2 * rows_q : 2 * rows_q + 1, :] for part in parts]
        best = functools.reduce(jnp.maximum, tops)
        factors = [jnp.exp(top - best) for top in tops]
        total = jnp.zeros((1, DH), F32)
        for f, part in zip(factors, parts):
            high, low = (part[2 * rows_q + i : 2 * rows_q + i + 1, :] for i in (1, 2))
            total = total + f * (high + low)
        scale = 1.0 / total
        normed = jnp.zeros((rows_q, DH), F32)
        for f, part in zip(factors, parts):
            weight = jnp.sum(jnp.where(mask, f * scale, 0.0), axis=1, keepdims=True)
            normed = normed + weight * (part[:rows_q, :] + part[rows_q : 2 * rows_q, :])
        for t in range(tokens):
            for h in range(HEADS):
                lines[t].append(normed[t * HEADS + h : t * HEADS + h + 1, :])
    rows = [jnp.concatenate(line, axis=1) for line in lines]
    out_ref[...] = jnp.concatenate(rows, axis=0).astype(BF16)


def ctx_kernel(xs, before, valid_ref, q_ref, k_ref, v_ref, *refs):
    anchors, refs = refs[: len(xs)], refs[len(xs) :]
    if before:
        _, out_hbm, bias_ref, keep_ref, out_ref, sems = refs
    else:
        out_hbm, mark_ref, bias_ref, keep_ref, out_ref, sems = refs
        mark_ref[...] = jnp.zeros(mark_ref.shape, F32)
    block = k_ref.shape[0]
    host = lax.axis_index("hst")
    me = lax.rem(host, KVH)
    count = valid_ref[0]
    row = lax.broadcasted_iota(jnp.int32, (block, block), 0)
    col = lax.broadcasted_iota(jnp.int32, (block, block), 1)
    bias_ref[:, :block] = jnp.broadcast_to(jnp.where(host > 0, 0.0, NEG), (block, block))
    bias_ref[:, block:] = jnp.where((col <= row) & (col < count), 0.0, NEG)
    keep_ref[...] = jnp.where(lax.broadcasted_iota(jnp.int32, (block, DH), 0) < count, 1.0, 0.0)
    wide = HEADS // 4 * DH
    copies = []
    for i, x in enumerate(xs):
        head = jnp.bitwise_xor(me, x)
        cols = head_columns(head)
        keys = jnp.concatenate([anchors[i][:block, :], k_ref[:, cols]], axis=0)
        values = jnp.concatenate([anchors[i][block:, :], v_ref[:, cols]], axis=0)
        for h in range(HEADS):
            at = pl.ds(pl.multiple_of(head * (HEADS * DH) + h * DH, DH), DH)
            s = dot_nt(q_ref[:, at], keys) * SCALE + bias_ref[...]
            best = jnp.max(s, axis=1, keepdims=True)
            e = jnp.exp(s - best)
            total = jnp.sum(e, axis=1, keepdims=True)
            mixed = dot_nn(e.astype(BF16), values)
            out_ref[i, :, h * DH : (h + 1) * DH] = (
                mixed * (keep_ref[...] * (1.0 / total))
            ).astype(BF16)
            if (h + 1) * DH % wide == 0:
                part = (h + 1) * DH // wide - 1
                to = pl.ds(pl.multiple_of(head * (HEADS * DH) + part * wide, wide), wide)
                copy = pltpu.make_async_copy(
                    out_ref.at[i, :, part * wide : (part + 1) * wide],
                    out_hbm.at[:, to],
                    sems.at[i, part],
                )
                copy.start()
                copies.append(copy)
    for copy in copies:
        copy.wait()


def ctx_call(valid, q, k, v, pieces, before=()):
    block, width = q.shape
    xs, anchors = zip(*pieces)
    operands = [valid, q, k, v, *anchors, *before]
    outs, specs = [jax.ShapeDtypeStruct(q.shape, BF16)], [HBM]
    if not before:
        outs, specs = outs + [jax.ShapeDtypeStruct((8, DH), F32)], specs + [VMEM]
    return pl.pallas_call(
        functools.partial(ctx_kernel, xs, bool(before)),
        out_shape=outs,
        in_specs=[SMEM] + [VMEM] * (3 + len(xs)) + [HBM] * len(before),
        out_specs=specs,
        scratch_shapes=[
            pltpu.VMEM((block, 2 * block), F32),
            pltpu.VMEM((block, DH), F32),
            pltpu.VMEM((len(xs), block, HEADS * DH), BF16),
            pltpu.SemaphoreType.DMA((len(xs), 4)),
        ],
        input_output_aliases={len(operands) - 1: 0} if before else {},
        compiler_params=params(),
        cost_estimate=pl.CostEstimate(flops=int(COSTS.get("ctx", 1)), bytes_accessed=1, transcendentals=0),
        name="ctx",
    )(*operands)


def after_kernel(in_ref, mark_ref, out_ref):
    del mark_ref
    out_ref[...] = in_ref[...]


def small_call(kernel, outs, ins, operands, name, scratch=(), mib=32, out_space=VMEM):
    return pl.pallas_call(
        kernel,
        out_shape=outs,
        in_specs=ins,
        out_specs=jax.tree.map(lambda _: out_space, outs),
        scratch_shapes=scratch,
        compiler_params=pltpu.CompilerParams(vmem_limit_bytes=mib * 2**20),
        cost_estimate=pl.CostEstimate(flops=int(COSTS.get(name, 1)), bytes_accessed=1, transcendentals=0),
        name=name,
    )(*operands)


def body(hosts, ctx_q, ctx_k, ctx_v, ask_q, ask_k, ask_v, valid):
    block = ctx_q.shape[0]
    tokens = ask_q.shape[0]
    groups = hosts // KVH
    rows_q = tokens * HEADS
    rows_all = KVH * (rows_q + 2 * tokens)
    shape = jax.ShapeDtypeStruct
    me = place()
    group = lax.axis_index("hst") // KVH

    def near(array, x):
        return lax.ppermute(array, "hst", [(i, i ^ x) for i in range(hosts)])

    def far(array, d):
        return lax.ppermute(array, "hst", [(i, i ^ (d * KVH)) for i in range(hosts)])

    def from_first(array, d):
        order = [0, *range(d, groups), *range(d - 1, 0, -1)]
        after = dict(zip(order, order[1:] + order[:1]))
        if d == 1:
            after = {a: a ^ 1 for a in range(groups)}
        return lax.ppermute(
            array, "hst", [(i, after[i // KVH] * KVH + i % KVH) for i in range(hosts)]
        )

    mark = small_call(gate_kernel, shape((8, DH), F32), [], (), "gate")
    packed = small_call(
        pack_kernel,
        [shape((rows_q + round_up(2 * tokens + 1, SUB), DH), BF16)] * KVH
        + [shape((2 * block, DH), BF16)] * KVH,
        [SMEM] + [VMEM] * 6,
        (valid, ask_q, ask_k, ask_v, ctx_k, ctx_v, mark),
        "pack",
    )
    qs = [packed[0]] + [near(packed[x], x) for x in range(1, KVH)]
    kvs = [packed[KVH]] + [near(packed[KVH + x], x) for x in range(1, KVH)]
    mine = small_call(
        functools.partial(regroup_kernel, tokens), shape((rows_all, DH), BF16), [VMEM] * KVH, qs, "regroup"
    )
    again = small_call(
        after_kernel, shape(mine.shape, BF16), [VMEM] * 2, (mine, kvs[1]), "again"
    )
    zs = [mine, far(again, 1)] + [far(mine, d) for d in range(2, groups)]

    anchor = kvs[0]
    for x in range(1, KVH):
        anchor = jnp.where(me == x, kvs[x], anchor)
    arrived = [from_first(anchor, d) for d in range(1, groups)]
    for d in range(1, groups):
        anchor = jnp.where(group == d, arrived[d - 1], anchor)
    parts = small_call(
        functools.partial(ask_kernel, hosts, tokens),
        shape((hosts, 2 * rows_q + 8, DH), BF16),
        [VMEM] * (groups + 2 * KVH),
        (*zs, *qs, *kvs),
        "ask",
    )
    parts = lax.all_to_all(parts, "hst", split_axis=0, concat_axis=0, tiled=True)
    half = KVH // 2
    context = functools.partial(ctx_call, valid, ctx_q, ctx_k, ctx_v)
    ctx_out, mark = context([(0, anchor)] + [(x, near(anchor, x)) for x in range(1, half)])
    second = small_call(
        after_kernel, shape(anchor.shape, BF16), [VMEM] * 2, (near(anchor, half), mark), "after"
    )
    pieces = [(half, second)] + [(half + x, near(second, x)) for x in range(1, half)]
    (ctx_out,) = context(pieces, (ctx_out,))
    ask_out = small_call(merge_kernel, shape(ask_q.shape, BF16), [VMEM], (parts,), "merge")
    return (ctx_out, ask_out)


def solution(mesh):
    rows = P(("req", "hst"), None)
    return jax.shard_map(
        functools.partial(body, mesh.shape["hst"]),
        mesh=mesh,
        in_specs=(rows,) * 6 + (P(("req", "hst")),),
        out_specs=(rows, rows),
        check_vma=False,
    )
```
